32 devices in a mesh: dp: 4 (over z), expert: 8 (over y, x, core).
Axes of the slice: x: 2, y: 2, z: 4, core: 2. Of those that a mesh axis runs over, the one named last changes fastest.
Arguments:
- tokens: bfloat16 [2048, 4096], P('expert', 'dp'), may hold values from -6 to 6
- targets: bfloat16 [2048, 4096], P('expert', 'dp'), may hold values from -4 to 4
- expert_ids: int32 [2048, 2], P('expert'), may hold values from 0 to 7, all different within a row; in each aligned block of 256 rows (0 to 255, 256 to 511, ...) at most 128 rows name the same one
- gate_weights: float32 [2048, 2], P('expert'), may hold values from 0.2 to 1
- level_weights: float32 [2048], P('expert'), may hold values from 0.2 to 2
- w_gate: bfloat16 [8, 4096, 1024], P('expert', 'dp'), may hold values from -0.09375 to 0.09375
- w_up: bfloat16 [8, 4096, 1024], P('expert', 'dp'), may hold values from -0.09375 to 0.09375
- w_down: bfloat16 [8, 1024, 4096], P('expert', None, 'dp'), may hold values from -0.1875 to 0.1875
Outputs:
- mixed: bfloat16 [2048, 4096], P('expert', 'dp')
- token_grad: bfloat16 [2048, 4096], P('expert', 'dp')
- gate_grads: float32 [8, 4096, 1024], P('expert', 'dp')
- up_grads: float32 [8, 4096, 1024], P('expert', 'dp')
- down_grads: float32 [8, 1024, 4096], P('expert', None, 'dp')
The draws below stay inside these ranges and needn't reach their ends.
Inputs may be any that keep to these rules, and one draw needn't show every extreme that they name: `expert_ids`: each row names two different experts. Among the rows of one device no expert is named more than 128 times, a bound that some block reaches.
All inputs are finite; a program needn't handle non-finite values.
Results may differ from the reference program's by a relative error of at most 0.0065.
Values may be sent and summed in bfloat16 or wider, within the bound.
A program may use at most 128 MiB of HBM per device.

```python
import math
import jax
import jax.numpy as jnp
import numpy as np
from jax import lax

D = 4096
FF = 1024
TOK_DEV = 256
EXPERTS = 8
CAP = 128
SLOTS = 1024
TOKENS = 2048
N_EXPERT = 8


def level_of(key, extent, split, smallest, high):
    def one(position, shards_of):
        draws = jax.random.uniform(jax.random.fold_in(jax.random.fold_in(key, 6), position), (shards_of,), jnp.float32, smallest / len(split), high / len(split))
        return jnp.repeat(jnp.exp(draws), extent[position] // shards_of).reshape((-1,) + (1,) * (len(extent) - position - 1))

    factor_of = one(*split[0])
    for cut in split[1:]:
        factor_of = factor_of * one(*cut)
    return factor_of


def routed_block(stream_key, own, number, rows, count, top, limit, slope):
    order = jax.random.permutation(stream_key, count)
    crowded, usual = load_shares(count, rows * top, limit, slope, True), load_shares(count, rows * top, limit, slope, False)
    places = jnp.arange(count)

    def named(lengths, turn):
        used = int((lengths > 0).sum())
        fixed = max(1, used // 4)
        shifted = fixed + (places - fixed + turn * (used - fixed)) % max(1, count - fixed)
        return jnp.zeros((count,), jnp.int32).at[order[jnp.where(places < fixed, places, shifted)]].set(jnp.asarray(lengths, jnp.int32))

    lengths = jnp.where(number % 4 == 0, named(crowded, number // 4), named(usual, number - number // 4 - 1))
    mixed = jax.random.permutation(jax.random.fold_in(own, 3), count)
    source_of, receiver = mixed[0:count // 2 * 2:2], mixed[1:count // 2 * 2:2]
    slack = jnp.minimum(lengths[source_of] - 1, limit - lengths[receiver]) // 2
    slack = jnp.where((source_of == order[0]) | (receiver == order[0]) | (lengths[receiver] == 0), 0, jnp.maximum(slack, 0))
    shifted = jax.random.randint(jax.random.fold_in(own, 4), (count // 2,), 0, 1 << 20) % (slack + 1)
    lengths = lengths.at[source_of].add(-shifted).at[receiver].add(shifted)
    members = jnp.searchsorted(jnp.cumsum(lengths), jnp.arange(rows * top), side="right").astype(jnp.int32)
    table = members.reshape(top, rows).T
    table = table[jax.random.permutation(jax.random.fold_in(own, 1), rows)]
    turn = jax.random.randint(jax.random.fold_in(own, 2), (rows, 1), 0, top)
    return jnp.take_along_axis(table, (jnp.arange(top)[None, :] + turn) % top, axis=1)


def load_shares(number_of, total, reach, slope, full):
    weights = [(1 << 20) // math.isqrt(standing ** slope) + 1 for standing in range(1, number_of + 1)]
    largest = reach if full else min(reach, max(-(-total // number_of), total * weights[0] // sum(weights)))
    least = 1 if total - largest >= number_of - 1 else 0
    counts, surplus = [largest] + [least] * (number_of - 1), total - largest - least * (number_of - 1)
    while surplus > 0:
        free = [i for i in range(1, number_of) if counts[i] < largest] or [i for i in range(1, number_of) if counts[i] < reach]
        mass, remaining = sum([weights[i] for i in free]), surplus
        for i in free:
            addition = min(reach - counts[i], max(1, remaining * weights[i] // mass), surplus)
            counts[i] = counts[i] + addition
            surplus = surplus - addition
    return np.array(counts)


def normal_values(own_key, dims, scale, most, cuts=(), kind=jnp.bfloat16):
    drawn = scale * jax.random.normal(own_key, dims, jnp.float32)
    if cuts:
        drawn = drawn * level_of(own_key, dims, cuts, -0.22, 0.18)
    return jnp.clip(drawn, -most, most).astype(kind)


def setup_inputs(seed: int = 0) -> dict:
    key_of = jax.random.split(jax.random.key(seed), 9)
    tokens = normal_values(key_of[0], (TOKENS, D), 1.0, 6.0, ((0, 8), (1, 4)))
    targets = normal_values(key_of[1], (TOKENS, D), 0.5, 4.0, ((0, 8), (1, 4)))
    expert_ids_keys = jax.random.split(jax.random.fold_in(key_of[2], 1), TOKENS // TOK_DEV)
    expert_ids_turns = jax.random.permutation(jax.random.fold_in(key_of[2], 3), TOKENS // TOK_DEV)
    expert_ids = jax.vmap(lambda own, number: routed_block(jax.random.fold_in(key_of[2], 2), own, number, TOK_DEV, EXPERTS, 2, CAP, 2))(expert_ids_keys, expert_ids_turns).reshape((TOKENS, 2))
    gate_weights = jnp.clip(0.2 + 0.8 * jax.random.uniform(key_of[3], (TOKENS, 2), jnp.float32) ** level_of(key_of[3], (TOKENS, 2), ((0, 8),), -0.2, 0.2), 0.2, 1.0)
    level_weights = jnp.clip(jnp.exp(math.log(2.0) - 2.3025851 * jax.random.uniform(key_of[4], (TOKENS,), jnp.float32) ** level_of(key_of[4], (TOKENS,), ((0, 8),), -0.2, 0.2)), 0.2, 2.0)
    w_gate = normal_values(key_of[5], (EXPERTS, D, FF), D ** -0.5, 0.09375, ((0, 8), (1, 4)))
    w_up = normal_values(key_of[6], (EXPERTS, D, FF), D ** -0.5, 0.09375, ((0, 8), (1, 4)))
    w_down = normal_values(key_of[7], (EXPERTS, FF, D), FF ** -0.5, 0.1875, ((0, 8), (2, 4)))
    return {"tokens": tokens, "targets": targets, "expert_ids": expert_ids, "gate_weights": gate_weights, "level_weights": level_weights, "w_gate": w_gate, "w_up": w_up, "w_down": w_down}


def slot_ranks(routing, experts):
    listed = routing.reshape(routing.shape[0], -1)
    onehot = (listed[:, :, None] == jnp.arange(experts, dtype=jnp.int32)[None, None, :]).astype(jnp.int32)
    earlier = jnp.cumsum(onehot, axis=1) - onehot
    return jnp.sum(earlier * onehot, axis=2).astype(jnp.int32)


def reference(tokens, targets, expert_ids, gate_weights, level_weights, w_gate, w_up, w_down):
    routing = expert_ids.reshape(N_EXPERT, TOK_DEV, 2)
    ranks = slot_ranks(routing, EXPERTS).reshape(-1)
    listed = expert_ids.reshape(-1).astype(jnp.int32)
    blocks = (jnp.arange(2 * TOKENS, dtype=jnp.int32) // (2 * TOK_DEV)).astype(jnp.int32)
    places = (blocks * CAP + ranks).astype(jnp.int32)
    spread = jnp.repeat(tokens, 2, axis=0)

    def scatter_rows(values, which):
        chosen = jnp.where(listed == which, places, SLOTS)
        return jnp.zeros((SLOTS, D), jnp.bfloat16).at[chosen].set(values, mode="drop")

    def projections(which):
        inputs = scatter_rows(spread, which)
        gate_pre = jnp.dot(inputs, w_gate[which], preferred_element_type=jnp.float32)
        up_pre = jnp.dot(inputs, w_up[which], preferred_element_type=jnp.float32)
        sigmoid_gate = jax.nn.sigmoid(gate_pre)
        hidden = (gate_pre * sigmoid_gate * up_pre).astype(jnp.bfloat16)
        return inputs, gate_pre, up_pre, sigmoid_gate, hidden

    def forward(which):
        hidden = projections(which)[4]
        return jnp.dot(hidden, w_down[which], preferred_element_type=jnp.float32).astype(jnp.bfloat16)

    everyone = jnp.arange(EXPERTS, dtype=jnp.int32)
    outputs = lax.map(forward, everyone)
    picked = outputs[listed, places].reshape(TOKENS, 2, D).astype(jnp.float32)
    combined = jnp.sum(gate_weights[:, :, None] * picked, axis=1)
    mixed = combined.astype(jnp.bfloat16)
    row_grad = level_weights[:, None] * (combined - targets.astype(jnp.float32))
    slot_grad = (gate_weights[:, :, None] * row_grad[:, None, :]).astype(jnp.bfloat16).reshape(2 * TOKENS, D)

    def backward(which):
        inputs, gate_pre, up_pre, sigmoid_gate, hidden = projections(which)
        arrived = scatter_rows(slot_grad, which)
        hidden_grad = jnp.dot(arrived, w_down[which].T, preferred_element_type=jnp.float32)
        gate_delta = (hidden_grad * up_pre * sigmoid_gate * (1.0 + gate_pre * (1.0 - sigmoid_gate))).astype(jnp.bfloat16)
        up_delta = (hidden_grad * gate_pre * sigmoid_gate).astype(jnp.bfloat16)
        input_grad = (jnp.dot(gate_delta, w_gate[which].T, preferred_element_type=jnp.float32)
                      + jnp.dot(up_delta, w_up[which].T, preferred_element_type=jnp.float32)).astype(jnp.bfloat16)
        gate_grad = jnp.dot(inputs.T, gate_delta, preferred_element_type=jnp.float32)
        up_grad = jnp.dot(inputs.T, up_delta, preferred_element_type=jnp.float32)
        down_grad = jnp.dot(hidden.T, arrived, preferred_element_type=jnp.float32)
        return input_grad, gate_grad, up_grad, down_grad

    input_grads, gate_grads, up_grads, down_grads = lax.map(backward, everyone)
    picked_grads = input_grads[listed, places].reshape(TOKENS, 2, D).astype(jnp.float32)
    token_grad = jnp.sum(picked_grads, axis=1).astype(jnp.bfloat16)
    return (mixed, token_grad, gate_grads, up_grads, down_grads)
```

```python
import functools

import jax
import jax.numpy as jnp
from jax import lax
from jax.experimental import pallas as pl
from jax.experimental.pallas import tpu as pltpu
from jax.sharding import PartitionSpec as P

BF16 = jnp.bfloat16
F32 = jnp.float32
MESH = pl.DeviceIdType.MESH

DISPATCH, OUTPUT, GRAD, INPUT = range(4)
GATE, UP, HIDDEN, HIDDEN_GRAD, GATE_DELTA, UP_DELTA = range(6)


def contract(left, right, left_dim, right_dim):
    return lax.dot_general(
        left, right, (((left_dim,), (right_dim,)), ((), ())), preferred_element_type=F32
    )


def layer(
    n_z,
    n_e,
    cap,
    tok,
    tgt,
    slot_cols,
    slot_lanes,
    gate_w,
    level_w,
    w_gate,
    w_up,
    w_down,
    mixed,
    token_grad,
    gate_grad,
    up_grad,
    down_grad,
    stage,
    arrived,
    pre_out,
    pre_in,
    gate_own,
    up_own,
    hidden,
    returned,
    slot_grad,
    grads,
    grad_own,
    grad_in,
    gate_delta,
    up_delta,
    back,
    tiles,
    e_send,
    e_recv,
    z_send,
    z_recv,
    tile_sem,
):
    my_z = lax.axis_index("dp")
    my_e = lax.axis_index("expert")
    rows_all = n_e * cap
    shard = rows_all // n_z
    per_shard = n_e // n_z
    tok_rows = tok.shape[0]
    step = min(64, shard)

    def shard_rows(z):
        return pl.ds(pl.multiple_of(z * shard, shard), shard)

    def block_rows(e):
        return pl.ds(pl.multiple_of(e * cap, cap), cap)

    def e_copy(phase, landing, other, source):
        return pltpu.make_async_remote_copy(
            src_ref=stage.at[block_rows(other)],
            dst_ref=landing.at[block_rows(source)],
            send_sem=e_send.at[phase, other],
            recv_sem=e_recv.at[phase, source],
            device_id={"expert": other},
            device_id_type=MESH,
        )

    def send_blocks(phase, landing, z):
        for i in range(per_shard):
            other = z * per_shard + i

            @pl.when(other != my_e)
            def _():
                e_copy(phase, landing, other, my_e).start()

            @pl.when(other == my_e)
            def _():
                landing[block_rows(my_e), :] = stage[block_rows(my_e), :]

    def wait_blocks(phase, landing, z):
        for i in range(per_shard):
            other = z * per_shard + i

            @pl.when(other != my_e)
            def _():
                e_copy(phase, landing, other, other).wait_recv()

    def wait_sent(phase, landing):
        @pl.loop(0, n_e)
        def _(other):
            @pl.when(other != my_e)
            def _():
                e_copy(phase, landing, other, my_e).wait_send()

    def z_copy(phase, src, dst, z, source):
        return pltpu.make_async_remote_copy(
            src_ref=src,
            dst_ref=dst,
            send_sem=z_send.at[phase, z],
            recv_sem=z_recv.at[phase, source],
            device_id={"dp": z},
            device_id_type=MESH,
        )

    def gather_copy(phase, array, z, source):
        return z_copy(phase, array.at[shard_rows(source)], array.at[shard_rows(source)], z, source)

    def other_z(s):
        return lax.rem(my_z + s, n_z)

    barrier = pltpu.get_barrier_semaphore()

    @pl.loop(1, n_z)
    def _(s):
        pl.semaphore_signal(barrier, inc=1, device_id={"dp": other_z(s)}, device_id_type=MESH)

    @pl.loop(1, n_e)
    def _(s):
        pl.semaphore_signal(
            barrier, inc=1, device_id={"expert": lax.rem(my_e + s, n_e)}, device_id_type=MESH
        )

    pl.semaphore_wait(barrier, n_z + n_e - 2)

    def scatter_tile(z, k):
        slots = lax.broadcasted_iota(jnp.int32, (shard, tok_rows), 0) + z * shard
        return (slots == slot_lanes[k : k + 1, :]).astype(F32)

    def gather_matrix(k):
        slots = lax.broadcasted_iota(jnp.int32, (tok_rows, rows_all), 1)
        return (slots == slot_cols[:, k : k + 1]).astype(F32)

    @pl.loop(0, n_z)
    def _(s):
        z = other_z(s + 1)
        chosen = (scatter_tile(z, 0) + scatter_tile(z, 1)).astype(BF16)
        stage[shard_rows(z), :] = contract(chosen, tok[...], 1, 0).astype(BF16)
        send_blocks(DISPATCH, arrived, z)

    @pl.loop(1, n_z)
    def _(s):
        z = other_z(s)
        wait_blocks(DISPATCH, arrived, z)
        rows = arrived[shard_rows(z), :]
        pre_out[GATE, z] = contract(rows, w_gate[...], 1, 0).astype(BF16)
        z_copy(GATE, pre_out.at[GATE, z], pre_in.at[GATE, my_z], z, my_z).start()
        pre_out[UP, z] = contract(rows, w_up[...], 1, 0).astype(BF16)
        z_copy(UP, pre_out.at[UP, z], pre_in.at[UP, my_z], z, my_z).start()

    wait_blocks(DISPATCH, arrived, my_z)
    gate_own[...] = contract(arrived[shard_rows(my_z), :], w_gate[...], 1, 0)
    up_own[...] = contract(arrived[shard_rows(my_z), :], w_up[...], 1, 0)
    wait_sent(DISPATCH, arrived)

    @pl.loop(1, n_z)
    def _(s):
        z = other_z(s)
        for phase, own in ((GATE, gate_own), (UP, up_own)):
            z_copy(phase, pre_out.at[phase, z], pre_in.at[phase, z], z, z).wait_recv()

            @pl.loop(0, shard // step)
            def _(c):
                rows = pl.ds(pl.multiple_of(c * step, step), step)
                own[rows, :] = own[rows, :] + pre_in[phase, z, rows, :].astype(F32)

    @pl.loop(0, shard // step)
    def _(c):
        rows = pl.ds(pl.multiple_of(c * step, step), step)
        gate = gate_own[rows, :]
        value = gate * jax.nn.sigmoid(gate) * up_own[rows, :]
        target = pl.ds(pl.multiple_of(my_z * shard + c * step, step), step)
        hidden[target, :] = value.astype(BF16)

    @pl.loop(1, n_z)
    def _(s):
        gather_copy(HIDDEN, hidden, other_z(s), my_z).start()

    @pl.loop(0, n_z)
    def _(s):
        z = other_z(s)

        @pl.when(s > 0)
        def _():
            gather_copy(HIDDEN, hidden, z, z).wait_recv()

        stage[shard_rows(z), :] = contract(hidden[shard_rows(z), :], w_down[...], 1, 0).astype(BF16)
        send_blocks(OUTPUT, returned, z)

    @pl.loop(0, n_z)
    def _(z):
        wait_blocks(OUTPUT, returned, z)

    combined = gate_w[:, 0:1] * contract(gather_matrix(0).astype(BF16), returned[...], 1, 0)
    combined = combined + gate_w[:, 1:2] * contract(
        gather_matrix(1).astype(BF16), returned[...], 1, 0
    )
    mixed[...] = combined.astype(BF16)
    row_grad = level_w[...] * (combined - tgt[...].astype(F32))
    slot_grad[0] = (gate_w[:, 0:1] * row_grad).astype(BF16)
    slot_grad[1] = (gate_w[:, 1:2] * row_grad).astype(BF16)
    wait_sent(OUTPUT, returned)

    @pl.loop(0, n_z)
    def _(s):
        z = other_z(s + 1)
        value = contract(scatter_tile(z, 0).astype(BF16), slot_grad[0], 1, 0)
        value = value + contract(scatter_tile(z, 1).astype(BF16), slot_grad[1], 1, 0)
        stage[shard_rows(z), :] = value.astype(BF16)
        send_blocks(GRAD, grads, z)

    @pl.loop(1, n_z)
    def _(s):
        z = other_z(s)
        z_copy(GATE, pre_out.at[GATE, z], pre_in.at[GATE, my_z], z, my_z).wait_send()
        wait_blocks(GRAD, grads, z)
        pre_out[GATE, z] = contract(grads[shard_rows(z), :], w_down[...], 1, 1).astype(BF16)
        z_copy(HIDDEN_GRAD, pre_out.at[GATE, z], grad_in.at[my_z], z, my_z).start()

    wait_blocks(GRAD, grads, my_z)
    grad_own[...] = contract(grads[shard_rows(my_z), :], w_down[...], 1, 1)
    wait_sent(GRAD, grads)

    def tile_copy(result, c, size):
        rows = pl.ds(pl.multiple_of(c * size, size), size)
        slot = lax.rem(c, 2)
        return pltpu.make_async_copy(tiles.at[slot], result.at[rows], tile_sem.at[slot])

    def weight_grad(result, left, right):
        size = tiles.shape[1]
        count = left.shape[1] // size

        @pl.loop(0, count)
        def _(c):
            @pl.when(c >= 2)
            def _():
                tile_copy(result, c - 2, size).wait()

            columns = pl.ds(pl.multiple_of(c * size, size), size)
            tiles[lax.rem(c, 2)] = contract(left[:, columns], right[...], 0, 0)
            tile_copy(result, c, size).start()

        @pl.loop(max(count - 2, 0), count)
        def _(c):
            tile_copy(result, c, size).wait()

    weight_grad(down_grad, hidden, grads)

    @pl.loop(1, n_z)
    def _(s):
        z = other_z(s)
        z_copy(HIDDEN_GRAD, pre_out.at[GATE, z], grad_in.at[z], z, z).wait_recv()

        @pl.loop(0, shard // step)
        def _(c):
            rows = pl.ds(pl.multiple_of(c * step, step), step)
            grad_own[rows, :] = grad_own[rows, :] + grad_in[z, rows, :].astype(F32)

    @pl.loop(0, shard // step)
    def _(c):
        rows = pl.ds(pl.multiple_of(c * step, step), step)
        target = pl.ds(pl.multiple_of(my_z * shard + c * step, step), step)
        gate = gate_own[rows, :]
        grad = grad_own[rows, :]
        sigmoid = jax.nn.sigmoid(gate)
        delta = grad * up_own[rows, :] * sigmoid * (1.0 + gate * (1.0 - sigmoid))
        gate_delta[target, :] = delta.astype(BF16)
        up_delta[target, :] = (grad * gate * sigmoid).astype(BF16)

    @pl.loop(1, n_z)
    def _(s):
        gather_copy(GATE_DELTA, gate_delta, other_z(s), my_z).start()
        gather_copy(UP_DELTA, up_delta, other_z(s), my_z).start()

    @pl.loop(0, n_z)
    def _(s):
        z = other_z(s)

        @pl.when(s > 0)
        def _():
            gather_copy(GATE_DELTA, gate_delta, z, z).wait_recv()
            gather_copy(UP_DELTA, up_delta, z, z).wait_recv()

        value = contract(gate_delta[shard_rows(z), :], w_gate[...], 1, 1)
        value = value + contract(up_delta[shard_rows(z), :], w_up[...], 1, 1)
        stage[shard_rows(z), :] = value.astype(BF16)
        send_blocks(INPUT, back, z)

    weight_grad(gate_grad, arrived, gate_delta)
    weight_grad(up_grad, arrived, up_delta)

    @pl.loop(0, n_z)
    def _(z):
        wait_blocks(INPUT, back, z)

    both = (gather_matrix(0) + gather_matrix(1)).astype(BF16)
    token_grad[...] = contract(both, back[...], 1, 0).astype(BF16)
    wait_sent(INPUT, back)

    @pl.loop(1, n_z)
    def _(s):
        z = other_z(s)
        z_copy(UP, pre_out.at[UP, z], pre_in.at[UP, my_z], z, my_z).wait_send()
        z_copy(HIDDEN_GRAD, pre_out.at[GATE, z], grad_in.at[my_z], z, my_z).wait_send()
        gather_copy(HIDDEN, hidden, z, my_z).wait_send()
        gather_copy(GATE_DELTA, gate_delta, z, my_z).wait_send()
        gather_copy(UP_DELTA, up_delta, z, my_z).wait_send()


def shards(tokens, targets, expert_ids, gate_weights, level_weights, w_gate, w_up, w_down):
    n_e = lax.axis_size("expert")
    n_z = lax.axis_size("dp")
    tok_rows, quarter = tokens.shape
    ff = w_gate.shape[2]
    cap = 4 * tok_rows // n_e
    rows_all = n_e * cap
    shard = rows_all // n_z

    listed = expert_ids.reshape(-1)
    onehot = (listed[:, None] == jnp.arange(n_e, dtype=jnp.int32)[None, :]).astype(BF16)
    places = jnp.arange(2 * tok_rows, dtype=jnp.int32)
    before = (places[None, :] < places[:, None]).astype(BF16)
    earlier = contract(before, onehot, 1, 0)
    ranks = jnp.sum(earlier * onehot.astype(F32), axis=1).astype(jnp.int32)
    slots = (listed * cap + ranks).reshape(tok_rows, 2)

    vmem = pl.BlockSpec(memory_space=pltpu.VMEM)
    hbm = pl.BlockSpec(memory_space=pl.ANY)
    tile = min(256, quarter, ff)
    outs = pl.pallas_call(
        functools.partial(layer, n_z, n_e, cap),
        out_shape=(
            jax.ShapeDtypeStruct((tok_rows, quarter), BF16),
            jax.ShapeDtypeStruct((tok_rows, quarter), BF16),
            jax.ShapeDtypeStruct((quarter, ff), F32),
            jax.ShapeDtypeStruct((quarter, ff), F32),
            jax.ShapeDtypeStruct((ff, quarter), F32),
        ),
        in_specs=[vmem] * 9,
        out_specs=(vmem, vmem, hbm, hbm, hbm),
        scratch_shapes=[
            pltpu.VMEM((rows_all, quarter), BF16),
            pltpu.VMEM((rows_all, quarter), BF16),
            pltpu.VMEM((2, n_z, shard, ff), BF16),
            pltpu.VMEM((2, n_z, shard, ff), BF16),
            pltpu.VMEM((shard, ff), F32),
            pltpu.VMEM((shard, ff), F32),
            pltpu.VMEM((rows_all, ff), BF16),
            pltpu.VMEM((rows_all, quarter), BF16),
            pltpu.VMEM((2, tok_rows, quarter), BF16),
            pltpu.VMEM((rows_all, quarter), BF16),
            pltpu.VMEM((shard, ff), F32),
            pltpu.VMEM((n_z, shard, ff), BF16),
            pltpu.VMEM((rows_all, ff), BF16),
            pltpu.VMEM((rows_all, ff), BF16),
            pltpu.VMEM((rows_all, quarter), BF16),
            pltpu.VMEM((2, tile, max(ff, quarter)), F32),
            pltpu.SemaphoreType.DMA((4, n_e)),
            pltpu.SemaphoreType.DMA((4, n_e)),
            pltpu.SemaphoreType.DMA((6, n_z)),
            pltpu.SemaphoreType.DMA((6, n_z)),
            pltpu.SemaphoreType.DMA((2,)),
        ],
        compiler_params=pltpu.CompilerParams(
            collective_id=0, has_side_effects=True, vmem_limit_bytes=60 * 1024 * 1024
        ),
        cost_estimate=pl.CostEstimate(
            flops=18 * rows_all * quarter * ff, bytes_accessed=20 * quarter * ff, transcendentals=0
        ),
    )(
        tokens,
        targets,
        slots,
        slots.T,
        gate_weights,
        level_weights[:, None],
        w_gate[0],
        w_up[0],
        w_down[0],
    )
    mixed, token_grad, gate_grad, up_grad, down_grad = outs
    return (mixed, token_grad, gate_grad[None], up_grad[None], down_grad[None])


def solution(mesh):
    in_specs = (
        P("expert", "dp"),
        P("expert", "dp"),
        P("expert", None),
        P("expert", None),
        P("expert"),
        P("expert", "dp", None),
        P("expert", "dp", None),
        P("expert", None, "dp"),
    )
    out_specs = (
        P("expert", "dp"),
        P("expert", "dp"),
        P("expert", "dp", None),
        P("expert", "dp", None),
        P("expert", None, "dp"),
    )
    return jax.shard_map(shards, mesh=mesh, in_specs=in_specs, out_specs=out_specs, check_vma=False)
```

```python
import functools

import jax
import jax.numpy as jnp
from jax import lax
from jax.experimental import pallas as pl
from jax.experimental.pallas import tpu as pltpu
from jax.sharding import PartitionSpec as P

BF16 = jnp.bfloat16
F32 = jnp.float32
MESH = pl.DeviceIdType.MESH

HALVES = 2

DISPATCH, OUTPUT, GRAD, INPUT = range(4)
GATE, UP, HIDDEN, HIDDEN_GRAD, GATE_DELTA, UP_DELTA = range(6)


def contract(left, right, left_dim, right_dim):
    return lax.dot_general(
        left, right, (((left_dim,), (right_dim,)), ((), ())), preferred_element_type=F32
    )


def layer(
    n_z,
    n_e,
    cap,
    tok,
    tgt,
    slot_cols,
    slot_lanes,
    gate_w,
    level_w,
    w_gate,
    w_up,
    w_down,
    mixed,
    token_grad,
    gate_grad,
    up_grad,
    down_grad,
    stage,
    arrived,
    pre_out,
    pre_in,
    gate_own,
    up_own,
    hidden,
    returned,
    slot_grad,
    grads,
    grad_own,
    grad_in,
    gate_delta,
    up_delta,
    back,
    tiles,
    e_send,
    e_recv,
    z_send,
    z_recv,
    tile_sem,
):
    my_z = lax.axis_index("dp")
    my_e = lax.axis_index("expert")
    rows_all = n_e * cap
    part = cap // HALVES
    half_rows = n_e * part
    shard = half_rows // n_z
    per_shard = n_e // n_z
    tok_rows = tok.shape[0]
    step = min(64, shard)

    def shard_rows(h, z):
        return pl.ds(pl.multiple_of(h * half_rows + z * shard, shard), shard)

    def block_rows(h, e):
        return pl.ds(pl.multiple_of(h * half_rows + e * part, part), part)

    def e_copy(phase, h, landing, other, source):
        return pltpu.make_async_remote_copy(
            src_ref=stage.at[block_rows(h, other)],
            dst_ref=landing.at[block_rows(h, source)],
            send_sem=e_send.at[phase, h, other],
            recv_sem=e_recv.at[phase, h, source],
            device_id={"expert": other},
            device_id_type=MESH,
        )

    def send_blocks(phase, h, landing, z):
        for i in range(per_shard):
            other = z * per_shard + i

            @pl.when(other != my_e)
            def _():
                e_copy(phase, h, landing, other, my_e).start()

            @pl.when(other == my_e)
            def _():
                landing[block_rows(h, my_e), :] = stage[block_rows(h, my_e), :]

    def wait_blocks(phase, h, landing, z):
        for i in range(per_shard):
            other = z * per_shard + i

            @pl.when(other != my_e)
            def _():
                e_copy(phase, h, landing, other, other).wait_recv()

    def wait_sent(phase, h, landing):
        @pl.loop(0, n_e)
        def _(other):
            @pl.when(other != my_e)
            def _():
                e_copy(phase, h, landing, other, my_e).wait_send()

    def z_copy(phase, h, src, dst, z, source):
        return pltpu.make_async_remote_copy(
            src_ref=src,
            dst_ref=dst,
            send_sem=z_send.at[phase, h, z],
            recv_sem=z_recv.at[phase, h, source],
            device_id={"dp": z},
            device_id_type=MESH,
        )

    def gather_copy(phase, h, array, z, source):
        rows = array.at[shard_rows(h, source)]
        return z_copy(phase, h, rows, rows, z, source)

    def sum_copy(phase, h, z, source):
        if phase == HIDDEN_GRAD:
            return z_copy(phase, h, pre_out.at[GATE, h, z], grad_in.at[h, source], z, source)
        return z_copy(phase, h, pre_out.at[phase, h, z], pre_in.at[phase, h, source], z, source)

    def other_z(s):
        return lax.rem(my_z + s, n_z)

    barrier = pltpu.get_barrier_semaphore()

    @pl.loop(1, n_z)
    def _(s):
        pl.semaphore_signal(barrier, inc=1, device_id={"dp": other_z(s)}, device_id_type=MESH)

    @pl.loop(1, n_e)
    def _(s):
        pl.semaphore_signal(
            barrier, inc=1, device_id={"expert": lax.rem(my_e + s, n_e)}, device_id_type=MESH
        )

    pl.semaphore_wait(barrier, n_z + n_e - 2)

    def scatter_tile(h, z, k):
        first = h * half_rows + z * shard
        slots = lax.broadcasted_iota(jnp.int32, (shard, tok_rows), 0) + first
        return (slots == slot_lanes[k : k + 1, :]).astype(F32)

    def gather_matrix(k):
        slots = lax.broadcasted_iota(jnp.int32, (tok_rows, rows_all), 1)
        return (slots == slot_cols[:, k : k + 1]).astype(F32)

    for h in range(HALVES):

        @pl.loop(0, n_z)
        def _(s):
            z = other_z(s + 1)
            chosen = (scatter_tile(h, z, 0) + scatter_tile(h, z, 1)).astype(BF16)
            stage[shard_rows(h, z), :] = contract(chosen, tok[...], 1, 0).astype(BF16)
            send_blocks(DISPATCH, h, arrived, z)

    for h in range(HALVES):

        @pl.loop(1, n_z)
        def _(s):
            z = other_z(s)
            wait_blocks(DISPATCH, h, arrived, z)
            rows = arrived[shard_rows(h, z), :]
            pre_out[GATE, h, z] = contract(rows, w_gate[...], 1, 0).astype(BF16)
            sum_copy(GATE, h, z, my_z).start()
            pre_out[UP, h, z] = contract(rows, w_up[...], 1, 0).astype(BF16)
            sum_copy(UP, h, z, my_z).start()

        wait_blocks(DISPATCH, h, arrived, my_z)
        gate_own[h] = contract(arrived[shard_rows(h, my_z), :], w_gate[...], 1, 0)
        up_own[h] = contract(arrived[shard_rows(h, my_z), :], w_up[...], 1, 0)

    def add_arrived(phase, h, own, landing):
        @pl.loop(1, n_z)
        def _(s):
            z = other_z(s)
            sum_copy(phase, h, z, z).wait_recv()

            @pl.loop(0, shard // step)
            def _(c):
                rows = pl.ds(pl.multiple_of(c * step, step), step)
                own[h, rows, :] = own[h, rows, :] + landing[h, z, rows, :].astype(F32)

    for h in range(HALVES):
        add_arrived(GATE, h, gate_own, pre_in.at[GATE])
        add_arrived(UP, h, up_own, pre_in.at[UP])

        @pl.loop(0, shard // step)
        def _(c):
            rows = pl.ds(pl.multiple_of(c * step, step), step)
            gate = gate_own[h, rows, :]
            value = gate * jax.nn.sigmoid(gate) * up_own[h, rows, :]
            first = h * half_rows + my_z * shard + c * step
            hidden[pl.ds(pl.multiple_of(first, step), step), :] = value.astype(BF16)

        @pl.loop(1, n_z)
        def _(s):
            gather_copy(HIDDEN, h, hidden, other_z(s), my_z).start()

    for h in range(HALVES):
        wait_sent(DISPATCH, h, arrived)

        @pl.loop(0, n_z)
        def _(s):
            z = other_z(s)

            @pl.when(s > 0)
            def _():
                gather_copy(HIDDEN, h, hidden, z, z).wait_recv()

            rows = hidden[shard_rows(h, z), :]
            stage[shard_rows(h, z), :] = contract(rows, w_down[...], 1, 0).astype(BF16)
            send_blocks(OUTPUT, h, returned, z)

    for h in range(HALVES):

        @pl.loop(0, n_z)
        def _(z):
            wait_blocks(OUTPUT, h, returned, z)

    combined = gate_w[:, 0:1] * contract(gather_matrix(0).astype(BF16), returned[...], 1, 0)
    combined = combined + gate_w[:, 1:2] * contract(
        gather_matrix(1).astype(BF16), returned[...], 1, 0
    )
    mixed[...] = combined.astype(BF16)
    row_grad = level_w[...] * (combined - tgt[...].astype(F32))
    slot_grad[0] = (gate_w[:, 0:1] * row_grad).astype(BF16)
    slot_grad[1] = (gate_w[:, 1:2] * row_grad).astype(BF16)

    for h in range(HALVES):
        wait_sent(OUTPUT, h, returned)

        @pl.loop(0, n_z)
        def _(s):
            z = other_z(s + 1)
            value = contract(scatter_tile(h, z, 0).astype(BF16), slot_grad[0], 1, 0)
            value = value + contract(scatter_tile(h, z, 1).astype(BF16), slot_grad[1], 1, 0)
            stage[shard_rows(h, z), :] = value.astype(BF16)
            send_blocks(GRAD, h, grads, z)

    for h in range(HALVES):

        @pl.loop(1, n_z)
        def _(s):
            z = other_z(s)
            sum_copy(GATE, h, z, my_z).wait_send()
            wait_blocks(GRAD, h, grads, z)
            rows = grads[shard_rows(h, z), :]
            pre_out[GATE, h, z] = contract(rows, w_down[...], 1, 1).astype(BF16)
            sum_copy(HIDDEN_GRAD, h, z, my_z).start()

        wait_blocks(GRAD, h, grads, my_z)
        grad_own[h] = contract(grads[shard_rows(h, my_z), :], w_down[...], 1, 1)

    def tile_copy(result, c, size):
        rows = pl.ds(pl.multiple_of(c * size, size), size)
        slot = lax.rem(c, 2)
        return pltpu.make_async_copy(tiles.at[slot], result.at[rows], tile_sem.at[slot])

    def weight_grad(result, left, right):
        size = tiles.shape[1]
        count = left.shape[1] // size

        @pl.loop(0, count)
        def _(c):
            @pl.when(c >= 2)
            def _():
                tile_copy(result, c - 2, size).wait()

            columns = pl.ds(pl.multiple_of(c * size, size), size)
            tiles[lax.rem(c, 2)] = contract(left[:, columns], right[...], 0, 0)
            tile_copy(result, c, size).start()

        @pl.loop(max(count - 2, 0), count)
        def _(c):
            tile_copy(result, c, size).wait()

    weight_grad(down_grad, hidden, grads)

    for h in range(HALVES):
        add_arrived(HIDDEN_GRAD, h, grad_own, grad_in)

        @pl.loop(0, shard // step)
        def _(c):
            rows = pl.ds(pl.multiple_of(c * step, step), step)
            first = h * half_rows + my_z * shard + c * step
            target = pl.ds(pl.multiple_of(first, step), step)
            gate = gate_own[h, rows, :]
            grad = grad_own[h, rows, :]
            sigmoid = jax.nn.sigmoid(gate)
            delta = grad * up_own[h, rows, :] * sigmoid * (1.0 + gate * (1.0 - sigmoid))
            gate_delta[target, :] = delta.astype(BF16)
            up_delta[target, :] = (grad * gate * sigmoid).astype(BF16)

        @pl.loop(1, n_z)
        def _(s):
            gather_copy(GATE_DELTA, h, gate_delta, other_z(s), my_z).start()
            gather_copy(UP_DELTA, h, up_delta, other_z(s), my_z).start()

    for h in range(HALVES):
        wait_sent(GRAD, h, grads)

        @pl.loop(0, n_z)
        def _(s):
            z = other_z(s)

            @pl.when(s > 0)
            def _():
                gather_copy(GATE_DELTA, h, gate_delta, z, z).wait_recv()
                gather_copy(UP_DELTA, h, up_delta, z, z).wait_recv()

            value = contract(gate_delta[shard_rows(h, z), :], w_gate[...], 1, 1)
            value = value + contract(up_delta[shard_rows(h, z), :], w_up[...], 1, 1)
            stage[shard_rows(h, z), :] = value.astype(BF16)
            send_blocks(INPUT, h, back, z)

    weight_grad(gate_grad, arrived, gate_delta)
    weight_grad(up_grad, arrived, up_delta)

    for h in range(HALVES):

        @pl.loop(0, n_z)
        def _(z):
            wait_blocks(INPUT, h, back, z)

    both = (gather_matrix(0) + gather_matrix(1)).astype(BF16)
    token_grad[...] = contract(both, back[...], 1, 0).astype(BF16)

    for h in range(HALVES):
        wait_sent(INPUT, h, back)

        @pl.loop(1, n_z)
        def _(s):
            z = other_z(s)
            sum_copy(UP, h, z, my_z).wait_send()
            sum_copy(HIDDEN_GRAD, h, z, my_z).wait_send()
            gather_copy(HIDDEN, h, hidden, z, my_z).wait_send()
            gather_copy(GATE_DELTA, h, gate_delta, z, my_z).wait_send()
            gather_copy(UP_DELTA, h, up_delta, z, my_z).wait_send()


def shards(tokens, targets, expert_ids, gate_weights, level_weights, w_gate, w_up, w_down):
    n_e = lax.axis_size("expert")
    n_z = lax.axis_size("dp")
    tok_rows, quarter = tokens.shape
    ff = w_gate.shape[2]
    cap = 4 * tok_rows // n_e
    rows_all = n_e * cap
    part = cap // HALVES
    shard = n_e * part // n_z

    listed = expert_ids.reshape(-1)
    onehot = (listed[:, None] == jnp.arange(n_e, dtype=jnp.int32)[None, :]).astype(BF16)
    places = jnp.arange(2 * tok_rows, dtype=jnp.int32)
    before = (places[None, :] < places[:, None]).astype(BF16)
    earlier = contract(before, onehot, 1, 0)
    ranks = jnp.sum(earlier * onehot.astype(F32), axis=1).astype(jnp.int32)
    slots = ranks // part * (n_e * part) + listed * part + ranks % part
    slots = slots.reshape(tok_rows, 2)

    vmem = pl.BlockSpec(memory_space=pltpu.VMEM)
    hbm = pl.BlockSpec(memory_space=pl.ANY)
    tile = min(256, quarter, ff)
    outs = pl.pallas_call(
        functools.partial(layer, n_z, n_e, cap),
        out_shape=(
            jax.ShapeDtypeStruct((tok_rows, quarter), BF16),
            jax.ShapeDtypeStruct((tok_rows, quarter), BF16),
            jax.ShapeDtypeStruct((quarter, ff), F32),
            jax.ShapeDtypeStruct((quarter, ff), F32),
            jax.ShapeDtypeStruct((ff, quarter), F32),
        ),
        in_specs=[vmem] * 9,
        out_specs=(vmem, vmem, hbm, hbm, hbm),
        scratch_shapes=[
            pltpu.VMEM((rows_all, quarter), BF16),
            pltpu.VMEM((rows_all, quarter), BF16),
            pltpu.VMEM((2, HALVES, n_z, shard, ff), BF16),
            pltpu.VMEM((2, HALVES, n_z, shard, ff), BF16),
            pltpu.VMEM((HALVES, shard, ff), F32),
            pltpu.VMEM((HALVES, shard, ff), F32),
            pltpu.VMEM((rows_all, ff), BF16),
            pltpu.VMEM((rows_all, quarter), BF16),
            pltpu.VMEM((2, tok_rows, quarter), BF16),
            pltpu.VMEM((rows_all, quarter), BF16),
            pltpu.VMEM((HALVES, shard, ff), F32),
            pltpu.VMEM((HALVES, n_z, shard, ff), BF16),
            pltpu.VMEM((rows_all, ff), BF16),
            pltpu.VMEM((rows_all, ff), BF16),
            pltpu.VMEM((rows_all, quarter), BF16),
            pltpu.VMEM((2, tile, max(ff, quarter)), F32),
            pltpu.SemaphoreType.DMA((4, HALVES, n_e)),
            pltpu.SemaphoreType.DMA((4, HALVES, n_e)),
            pltpu.SemaphoreType.DMA((6, HALVES, n_z)),
            pltpu.SemaphoreType.DMA((6, HALVES, n_z)),
            pltpu.SemaphoreType.DMA((2,)),
        ],
        compiler_params=pltpu.CompilerParams(
            collective_id=0, has_side_effects=True, vmem_limit_bytes=60 * 1024 * 1024
        ),
        cost_estimate=pl.CostEstimate(
            flops=18 * rows_all * quarter * ff, bytes_accessed=20 * quarter * ff, transcendentals=0
        ),
    )(
        tokens,
        targets,
        slots,
        slots.T,
        gate_weights,
        level_weights[:, None],
        w_gate[0],
        w_up[0],
        w_down[0],
    )
    mixed, token_grad, gate_grad, up_grad, down_grad = outs
    return (mixed, token_grad, gate_grad[None], up_grad[None], down_grad[None])


def solution(mesh):
    in_specs = (
        P("expert", "dp"),
        P("expert", "dp"),
        P("expert", None),
        P("expert", None),
        P("expert"),
        P("expert", "dp", None),
        P("expert", "dp", None),
        P("expert", None, "dp"),
    )
    out_specs = (
        P("expert", "dp"),
        P("expert", "dp"),
        P("expert", "dp", None),
        P("expert", "dp", None),
        P("expert", None, "dp"),
    )
    return jax.shard_map(shards, mesh=mesh, in_specs=in_specs, out_specs=out_specs, check_vma=False)
```

```python
import functools

import jax
import jax.numpy as jnp
from jax import lax
from jax.experimental import pallas as pl
from jax.experimental.pallas import tpu as pltpu
from jax.sharding import PartitionSpec as P

BF16 = jnp.bfloat16
F32 = jnp.float32
MESH = pl.DeviceIdType.MESH

HALVES = 2

DISPATCH, OUTPUT, GRAD, INPUT = range(4)
GATE, UP, HIDDEN, HIDDEN_GRAD, GATE_DELTA, UP_DELTA = range(6)


def contract(left, right, left_dim, right_dim):
    return lax.dot_general(
        left, right, (((left_dim,), (right_dim,)), ((), ())), preferred_element_type=F32
    )


def layer(
    n_z,
    n_e,
    cap,
    tok,
    tgt,
    slot_cols,
    slot_lanes,
    gate_w,
    level_w,
    w_gate,
    w_up,
    w_down,
    mixed,
    token_grad,
    gate_grad,
    up_grad,
    down_grad,
    stage,
    arrived,
    pre_out,
    pre_in,
    gate_own,
    up_own,
    hidden,
    returned,
    slot_grad,
    grads,
    grad_own,
    grad_in,
    gate_delta,
    up_delta,
    back,
    relay_in,
    tiles,
    e_send,
    e_recv,
    z_send,
    z_recv,
    relay_recv,
    tile_sem,
):
    my_z = lax.axis_index("dp")
    my_e = lax.axis_index("expert")
    rows_all = n_e * cap
    part = cap // HALVES
    half_rows = n_e * part
    shard = half_rows // n_z
    per_shard = n_e // n_z
    tok_rows = tok.shape[0]
    step = min(64, shard)

    def shard_rows(h, z):
        return pl.ds(pl.multiple_of(h * half_rows + z * shard, shard), shard)

    def block_rows(h, e):
        return pl.ds(pl.multiple_of(h * half_rows + e * part, part), part)

    def e_copy(phase, h, landing, other, source):
        return pltpu.make_async_remote_copy(
            src_ref=stage.at[block_rows(h, other)],
            dst_ref=landing.at[block_rows(h, source)],
            send_sem=e_send.at[phase, h, other],
            recv_sem=e_recv.at[phase, h, source],
            device_id={"expert": other},
            device_id_type=MESH,
        )

    def send_blocks(phase, h, landing, z):
        for i in range(per_shard):
            other = z * per_shard + i

            @pl.when(other != my_e)
            def _():
                e_copy(phase, h, landing, other, my_e).start()

            @pl.when(other == my_e)
            def _():
                landing[block_rows(h, my_e), :] = stage[block_rows(h, my_e), :]

    def wait_blocks(phase, h, landing, z):
        for i in range(per_shard):
            other = z * per_shard + i

            @pl.when(other != my_e)
            def _():
                e_copy(phase, h, landing, other, other).wait_recv()

    def wait_sent(phase, h, landing):
        @pl.loop(0, n_e)
        def _(other):
            @pl.when(other != my_e)
            def _():
                e_copy(phase, h, landing, other, my_e).wait_send()

    def z_copy(phase, h, src, dst, z, source):
        return pltpu.make_async_remote_copy(
            src_ref=src,
            dst_ref=dst,
            send_sem=z_send.at[phase, h, z],
            recv_sem=z_recv.at[phase, h, source],
            device_id={"dp": z},
            device_id_type=MESH,
        )

    def gather_copy(phase, h, array, z, source):
        rows = array.at[shard_rows(h, source)]
        return z_copy(phase, h, rows, rows, z, source)

    def sum_copy(phase, h, z, source):
        if phase == HIDDEN_GRAD:
            return z_copy(phase, h, pre_out.at[GATE, h, z], grad_in.at[h, source], z, source)
        return z_copy(phase, h, pre_out.at[phase, h, z], pre_in.at[phase, h, source], z, source)

    def other_z(s):
        return lax.rem(my_z + s, n_z)

    relay = n_z == 4

    def send_place(i):
        if not relay:
            return other_z(i + 1)
        upper, last = my_z // 2, i // 2
        return other_z((1 - last) * (3 - 2 * upper + lax.rem(i, 2) * (4 * upper - 2)) + 2 * last)

    def far(z):
        return (my_z - z) * (my_z - z) == 9

    def relay_copy(phase, h, z):
        slot = 2 if phase == HIDDEN_GRAD else phase
        return pltpu.make_async_remote_copy(
            src_ref=pre_out.at[phase % HIDDEN_GRAD, h, z],
            dst_ref=relay_in.at[slot, h],
            send_sem=z_send.at[phase, h, z],
            recv_sem=relay_recv.at[slot, h],
            device_id={"dp": 1 + my_z // 3},
            device_id_type=MESH,
        )

    def send_sum(phase, h, i, z, value):
        out = pre_out.at[phase % HIDDEN_GRAD, h, z]
        if not relay:
            out[...] = value.astype(BF16)
            sum_copy(phase, h, z, my_z).start()
            return
        adds = (i // 2) * lax.rem(my_z, 3)

        @pl.when(adds == 0)
        def _():
            out[...] = value.astype(BF16)

        @pl.when(adds != 0)
        def _():
            relay_copy(phase, h, z).wait_recv()
            slot = 2 if phase == HIDDEN_GRAD else phase
            out[...] = (value + relay_in[slot, h].astype(F32)).astype(BF16)

        @pl.when(far(z))
        def _():
            relay_copy(phase, h, z).start()

        @pl.when(jnp.logical_not(far(z)))
        def _():
            sum_copy(phase, h, z, my_z).start()

    barrier = pltpu.get_barrier_semaphore()

    @pl.loop(1, n_z)
    def _(s):
        pl.semaphore_signal(barrier, inc=1, device_id={"dp": other_z(s)}, device_id_type=MESH)

    @pl.loop(1, n_e)
    def _(s):
        pl.semaphore_signal(
            barrier, inc=1, device_id={"expert": lax.rem(my_e + s, n_e)}, device_id_type=MESH
        )

    pl.semaphore_wait(barrier, n_z + n_e - 2)

    def scatter_tile(h, z, k):
        first = h * half_rows + z * shard
        slots = lax.broadcasted_iota(jnp.int32, (shard, tok_rows), 0) + first
        return (slots == slot_lanes[k : k + 1, :]).astype(F32)

    def gather_matrix(k):
        slots = lax.broadcasted_iota(jnp.int32, (tok_rows, rows_all), 1)
        return (slots == slot_cols[:, k : k + 1]).astype(F32)

    for h in range(HALVES):

        @pl.loop(0, n_z)
        def _(s):
            z = other_z(s + 1)
            chosen = (scatter_tile(h, z, 0) + scatter_tile(h, z, 1)).astype(BF16)
            stage[shard_rows(h, z), :] = contract(chosen, tok[...], 1, 0).astype(BF16)
            send_blocks(DISPATCH, h, arrived, z)

    for h in range(HALVES):

        @pl.loop(0, n_z - 1)
        def _(i):
            z = send_place(i)
            wait_blocks(DISPATCH, h, arrived, z)
            rows = arrived[shard_rows(h, z), :]
            send_sum(GATE, h, i, z, contract(rows, w_gate[...], 1, 0))
            send_sum(UP, h, i, z, contract(rows, w_up[...], 1, 0))

        wait_blocks(DISPATCH, h, arrived, my_z)
        gate_own[h] = contract(arrived[shard_rows(h, my_z), :], w_gate[...], 1, 0)
        up_own[h] = contract(arrived[shard_rows(h, my_z), :], w_up[...], 1, 0)

    def add_arrived(phase, h, own, landing):
        @pl.loop(1, n_z)
        def _(s):
            z = other_z(s)

            @pl.when(jnp.logical_not(far(z)) if relay else s > 0)
            def _():
                sum_copy(phase, h, z, z).wait_recv()

                @pl.loop(0, shard // step)
                def _(c):
                    rows = pl.ds(pl.multiple_of(c * step, step), step)
                    own[h, rows, :] = own[h, rows, :] + landing[h, z, rows, :].astype(F32)

    for h in range(HALVES):
        add_arrived(GATE, h, gate_own, pre_in.at[GATE])
        add_arrived(UP, h, up_own, pre_in.at[UP])

        @pl.loop(0, shard // step)
        def _(c):
            rows = pl.ds(pl.multiple_of(c * step, step), step)
            gate = gate_own[h, rows, :]
            value = gate * jax.nn.sigmoid(gate) * up_own[h, rows, :]
            first = h * half_rows + my_z * shard + c * step
            hidden[pl.ds(pl.multiple_of(first, step), step), :] = value.astype(BF16)

        @pl.loop(1, n_z)
        def _(s):
            gather_copy(HIDDEN, h, hidden, other_z(s), my_z).start()

    for h in range(HALVES):
        wait_sent(DISPATCH, h, arrived)

        @pl.loop(0, n_z)
        def _(s):
            z = other_z(s)

            @pl.when(s > 0)
            def _():
                gather_copy(HIDDEN, h, hidden, z, z).wait_recv()

            rows = hidden[shard_rows(h, z), :]
            stage[shard_rows(h, z), :] = contract(rows, w_down[...], 1, 0).astype(BF16)
            send_blocks(OUTPUT, h, returned, z)

    for h in range(HALVES):

        @pl.loop(0, n_z)
        def _(z):
            wait_blocks(OUTPUT, h, returned, z)

    combined = gate_w[:, 0:1] * contract(gather_matrix(0).astype(BF16), returned[...], 1, 0)
    combined = combined + gate_w[:, 1:2] * contract(
        gather_matrix(1).astype(BF16), returned[...], 1, 0
    )
    mixed[...] = combined.astype(BF16)
    row_grad = level_w[...] * (combined - tgt[...].astype(F32))
    slot_grad[0] = (gate_w[:, 0:1] * row_grad).astype(BF16)
    slot_grad[1] = (gate_w[:, 1:2] * row_grad).astype(BF16)

    for h in range(HALVES):
        wait_sent(OUTPUT, h, returned)

        @pl.loop(0, n_z)
        def _(s):
            z = other_z(s + 1)
            value = contract(scatter_tile(h, z, 0).astype(BF16), slot_grad[0], 1, 0)
            value = value + contract(scatter_tile(h, z, 1).astype(BF16), slot_grad[1], 1, 0)
            stage[shard_rows(h, z), :] = value.astype(BF16)
            send_blocks(GRAD, h, grads, z)

    for h in range(HALVES):

        @pl.loop(0, n_z - 1)
        def _(i):
            z = send_place(i)
            sum_copy(GATE, h, z, my_z).wait_send()
            wait_blocks(GRAD, h, grads, z)
            rows = grads[shard_rows(h, z), :]
            send_sum(HIDDEN_GRAD, h, i, z, contract(rows, w_down[...], 1, 1))

        wait_blocks(GRAD, h, grads, my_z)
        grad_own[h] = contract(grads[shard_rows(h, my_z), :], w_down[...], 1, 1)

    def tile_copy(result, c, size):
        rows = pl.ds(pl.multiple_of(c * size, size), size)
        slot = lax.rem(c, 2)
        return pltpu.make_async_copy(tiles.at[slot], result.at[rows], tile_sem.at[slot])

    def weight_grad(result, left, right):
        size = tiles.shape[1]
        count = left.shape[1] // size

        @pl.loop(0, count)
        def _(c):
            @pl.when(c >= 2)
            def _():
                tile_copy(result, c - 2, size).wait()

            columns = pl.ds(pl.multiple_of(c * size, size), size)
            tiles[lax.rem(c, 2)] = contract(left[:, columns], right[...], 0, 0)
            tile_copy(result, c, size).start()

        @pl.loop(max(count - 2, 0), count)
        def _(c):
            tile_copy(result, c, size).wait()

    weight_grad(down_grad, hidden, grads)

    for h in range(HALVES):
        add_arrived(HIDDEN_GRAD, h, grad_own, grad_in)

        @pl.loop(0, shard // step)
        def _(c):
            rows = pl.ds(pl.multiple_of(c * step, step), step)
            first = h * half_rows + my_z * shard + c * step
            target = pl.ds(pl.multiple_of(first, step), step)
            gate = gate_own[h, rows, :]
            grad = grad_own[h, rows, :]
            sigmoid = jax.nn.sigmoid(gate)
            delta = grad * up_own[h, rows, :] * sigmoid * (1.0 + gate * (1.0 - sigmoid))
            gate_delta[target, :] = delta.astype(BF16)
            up_delta[target, :] = (grad * gate * sigmoid).astype(BF16)

        @pl.loop(1, n_z)
        def _(s):
            gather_copy(GATE_DELTA, h, gate_delta, other_z(s), my_z).start()
            gather_copy(UP_DELTA, h, up_delta, other_z(s), my_z).start()

    for h in range(HALVES):
        wait_sent(GRAD, h, grads)

        @pl.loop(0, n_z)
        def _(s):
            z = other_z(s)

            @pl.when(s > 0)
            def _():
                gather_copy(GATE_DELTA, h, gate_delta, z, z).wait_recv()
                gather_copy(UP_DELTA, h, up_delta, z, z).wait_recv()

            value = contract(gate_delta[shard_rows(h, z), :], w_gate[...], 1, 1)
            value = value + contract(up_delta[shard_rows(h, z), :], w_up[...], 1, 1)
            stage[shard_rows(h, z), :] = value.astype(BF16)
            send_blocks(INPUT, h, back, z)

    weight_grad(gate_grad, arrived, gate_delta)
    weight_grad(up_grad, arrived, up_delta)

    for h in range(HALVES):

        @pl.loop(0, n_z)
        def _(z):
            wait_blocks(INPUT, h, back, z)

    both = (gather_matrix(0) + gather_matrix(1)).astype(BF16)
    token_grad[...] = contract(both, back[...], 1, 0).astype(BF16)

    for h in range(HALVES):
        wait_sent(INPUT, h, back)

        @pl.loop(1, n_z)
        def _(s):
            z = other_z(s)
            sum_copy(UP, h, z, my_z).wait_send()
            sum_copy(HIDDEN_GRAD, h, z, my_z).wait_send()
            gather_copy(HIDDEN, h, hidden, z, my_z).wait_send()
            gather_copy(GATE_DELTA, h, gate_delta, z, my_z).wait_send()
            gather_copy(UP_DELTA, h, up_delta, z, my_z).wait_send()


def shards(tokens, targets, expert_ids, gate_weights, level_weights, w_gate, w_up, w_down):
    n_e = lax.axis_size("expert")
    n_z = lax.axis_size("dp")
    tok_rows, quarter = tokens.shape
    ff = w_gate.shape[2]
    cap = 4 * tok_rows // n_e
    rows_all = n_e * cap
    part = cap // HALVES
    shard = n_e * part // n_z

    listed = expert_ids.reshape(-1)
    onehot = (listed[:, None] == jnp.arange(n_e, dtype=jnp.int32)[None, :]).astype(BF16)
    places = jnp.arange(2 * tok_rows, dtype=jnp.int32)
    before = (places[None, :] < places[:, None]).astype(BF16)
    earlier = contract(before, onehot, 1, 0)
    ranks = jnp.sum(earlier * onehot.astype(F32), axis=1).astype(jnp.int32)
    slots = ranks // part * (n_e * part) + listed * part + ranks % part
    slots = slots.reshape(tok_rows, 2)

    vmem = pl.BlockSpec(memory_space=pltpu.VMEM)
    hbm = pl.BlockSpec(memory_space=pl.ANY)
    tile = min(256, quarter, ff)
    outs = pl.pallas_call(
        functools.partial(layer, n_z, n_e, cap),
        out_shape=(
            jax.ShapeDtypeStruct((tok_rows, quarter), BF16),
            jax.ShapeDtypeStruct((tok_rows, quarter), BF16),
            jax.ShapeDtypeStruct((quarter, ff), F32),
            jax.ShapeDtypeStruct((quarter, ff), F32),
            jax.ShapeDtypeStruct((ff, quarter), F32),
        ),
        in_specs=[vmem] * 9,
        out_specs=(vmem, vmem, hbm, hbm, hbm),
        scratch_shapes=[
            pltpu.VMEM((rows_all, quarter), BF16),
            pltpu.VMEM((rows_all, quarter), BF16),
            pltpu.VMEM((2, HALVES, n_z, shard, ff), BF16),
            pltpu.VMEM((2, HALVES, n_z, shard, ff), BF16),
            pltpu.VMEM((HALVES, shard, ff), F32),
            pltpu.VMEM((HALVES, shard, ff), F32),
            pltpu.VMEM((rows_all, ff), BF16),
            pltpu.VMEM((rows_all, quarter), BF16),
            pltpu.VMEM((2, tok_rows, quarter), BF16),
            pltpu.VMEM((rows_all, quarter), BF16),
            pltpu.VMEM((HALVES, shard, ff), F32),
            pltpu.VMEM((HALVES, n_z, shard, ff), BF16),
            pltpu.VMEM((rows_all, ff), BF16),
            pltpu.VMEM((rows_all, ff), BF16),
            pltpu.VMEM((rows_all, quarter), BF16),
            pltpu.VMEM((3, HALVES, shard, ff), BF16),
            pltpu.VMEM((2, tile, max(ff, quarter)), F32),
            pltpu.SemaphoreType.DMA((4, HALVES, n_e)),
            pltpu.SemaphoreType.DMA((4, HALVES, n_e)),
            pltpu.SemaphoreType.DMA((6, HALVES, n_z)),
            pltpu.SemaphoreType.DMA((6, HALVES, n_z)),
            pltpu.SemaphoreType.DMA((3, HALVES)),
            pltpu.SemaphoreType.DMA((2,)),
        ],
        compiler_params=pltpu.CompilerParams(
            collective_id=0, has_side_effects=True, vmem_limit_bytes=60 * 1024 * 1024
        ),
        cost_estimate=pl.CostEstimate(
            flops=18 * rows_all * quarter * ff, bytes_accessed=20 * quarter * ff, transcendentals=0
        ),
    )(
        tokens,
        targets,
        slots,
        slots.T,
        gate_weights,
        level_weights[:, None],
        w_gate[0],
        w_up[0],
        w_down[0],
    )
    mixed, token_grad, gate_grad, up_grad, down_grad = outs
    return (mixed, token_grad, gate_grad[None], up_grad[None], down_grad[None])


def solution(mesh):
    in_specs = (
        P("expert", "dp"),
        P("expert", "dp"),
        P("expert", None),
        P("expert", None),
        P("expert"),
        P("expert", "dp", None),
        P("expert", "dp", None),
        P("expert", None, "dp"),
    )
    out_specs = (
        P("expert", "dp"),
        P("expert", "dp"),
        P("expert", "dp", None),
        P("expert", "dp", None),
        P("expert", None, "dp"),
    )
    return jax.shard_map(shards, mesh=mesh, in_specs=in_specs, out_specs=out_specs, check_vma=False)
```
